512 devices in a mesh: blk: 128 (over x_lo, z, y), pair: 4 (over x_hi, core).
Axes of the slice: x: 4 (x_hi: 2, x_lo: 2; x = x_hi * 2 + x_lo), y: 4, z: 16, core: 2. Of those that a mesh axis runs over, the one named last changes fastest.
Arguments:
- series: bfloat16 [1024, 4096], P(None, 'blk'), may hold values from -2000 to 2000
- assign: int32 [1024], replicated, may hold values from 0 to 1023, each once
Outputs:
- cross: float32 [128, 4, 16, 8, 8, 256], P('blk', 'pair')
- opposite: float32 [128, 8, 8, 256], P('blk', None, None, 'pair')
The draws below stay inside these ranges and needn't reach their ends.
Inputs may be any that keep to these rules, and one draw needn't show every extreme that they name: `assign`: a permutation of the 1024 probe ids.
All inputs are finite; a program needn't handle non-finite values.
Results may differ from the reference program's by a relative error of at most 0.0041.
Values may be sent and summed in bfloat16 or wider, within the bound.
A program may use at most 128 MiB of HBM per device.

```python
import math
import jax
import jax.numpy as jnp
from jax import lax

PB = 8
SAMPLES = 4096
BINS = 1024
HALF_LAG = 128
BLOCKS = 128
PROBES = 1024
GROUPS = 4
PER_GROUP = 16


def draw_series(key, part):
    key = jax.random.fold_in(key, 17)
    key_list = jax.random.split(key, 5)
    source = jnp.clip(jax.random.normal(key_list[0], (SAMPLES,), jnp.float32), -6.0, 6.0)
    delays = jax.random.randint(key_list[1], (PROBES,), 0, HALF_LAG, dtype=jnp.int32)
    positions = (jnp.arange(SAMPLES, dtype=jnp.int32)[None, :] - delays[:, None]) % SAMPLES
    common = source[positions]
    noise_part = jnp.clip(jax.random.normal(key_list[2], (PROBES, SAMPLES), jnp.float32), -6.0, 6.0)
    envelope = jnp.exp(jax.random.uniform(key_list[3], (SAMPLES,), jnp.float32, 0.0, math.log(10.0)))
    gains = jnp.exp(jax.random.uniform(key_list[4], (PROBES, 1), jnp.float32, 0.0, math.log(10.0)))
    return (gains * envelope[None, :] * (common + noise_part)).astype(jnp.bfloat16)


def setup_inputs(seed: int = 0) -> dict:
    splits = jax.random.split(jax.random.key(seed), 3)
    return {
        "series": draw_series(jax.random.fold_in(splits[2], 71), 0),
        "assign": jax.random.permutation(splits[1], PROBES).astype(jnp.int32),
    }


def spectra_table():
    time_index = jnp.arange(SAMPLES, dtype=jnp.int32)
    frequencies = jnp.arange(1, BINS + 1, dtype=jnp.int32)
    phases = time_index[:, None] * frequencies[None, :] % SAMPLES
    angles = phases.astype(jnp.float32) * jnp.float32(2.0 * math.pi / SAMPLES)
    norm_scale = 1.0 / math.sqrt(SAMPLES)
    table_whole = jnp.stack([jnp.cos(angles) * norm_scale, jnp.sin(angles) * norm_scale], axis=1)
    return table_whole.astype(jnp.bfloat16).reshape(SAMPLES, 2 * BINS)

def lags_table():
    frequencies = jnp.arange(1, BINS + 1, dtype=jnp.int32)
    shifts = jnp.arange(2 * HALF_LAG, dtype=jnp.int32) - HALF_LAG + SAMPLES
    phases = frequencies[:, None] * shifts[None, :] % SAMPLES
    angles = phases.astype(jnp.float32) * jnp.float32(2.0 * math.pi / SAMPLES)
    lag_parts = jnp.stack([jnp.cos(angles), -jnp.sin(angles)], axis=0)
    return lag_parts.astype(jnp.bfloat16).reshape(2 * BINS, 2 * HALF_LAG)

def pair_corr(left_unit, right_unit, lag_table):
    members = left_unit.shape[0]
    left_wide = left_unit.astype(jnp.float32)
    right_wide = right_unit.astype(jnp.float32)
    real_part = left_wide[:, None, 0, :] * right_wide[None, :, 0, :] + left_wide[:, None, 1, :] * right_wide[None, :, 1, :]
    imag_part = left_wide[:, None, 1, :] * right_wide[None, :, 0, :] - left_wide[:, None, 0, :] * right_wide[None, :, 1, :]
    cross_spec = jnp.stack([real_part, imag_part], axis=2).astype(jnp.bfloat16)
    cross_spec = cross_spec.reshape(members * members, 2 * BINS)
    result = jnp.dot(cross_spec.astype(jnp.float32), lag_table.astype(jnp.float32), precision=lax.Precision.HIGHEST)
    return result.reshape(members, members, lag_table.shape[1])

def reference(series, assign):
    table_full = spectra_table().astype(jnp.float32)
    spectrum = jnp.dot(series.astype(jnp.float32), table_full, precision=lax.Precision.HIGHEST)
    spectrum = spectrum.reshape(PROBES, 2, BINS)
    energy = lax.optimization_barrier(jnp.sum(spectrum * spectrum, axis=(1, 2)))
    unit_rows = (spectrum * lax.rsqrt(energy + 1e-06)[:, None, None]).astype(jnp.bfloat16)
    blocks = unit_rows[assign].reshape(BLOCKS, PB, 2, BINS)
    lag_table = lags_table()
    round_steps = jnp.arange(PER_GROUP, dtype=jnp.int32)
    group_index = jnp.arange(GROUPS, dtype=jnp.int32)

    def per_block(block_index):
        own_unit = blocks[block_index]
        partners = (block_index + PER_GROUP * group_index[:, None] + round_steps[None, :]) % BLOCKS
        flat_partners = partners.reshape(-1).astype(jnp.int32)
        row_results = lax.map(lambda partner_one: pair_corr(own_unit, blocks[partner_one], lag_table), flat_partners)
        far_result = pair_corr(own_unit, blocks[(block_index + BLOCKS // 2) % BLOCKS], lag_table)
        return (row_results.reshape(GROUPS, PER_GROUP, PB, PB, 2 * HALF_LAG), far_result)
    cross_all, opposite_all = lax.map(per_block, jnp.arange(BLOCKS, dtype=jnp.int32))
    return (cross_all, opposite_all)
```

```python
import math

import jax
import jax.numpy as jnp
import ml_dtypes
import numpy as np
from jax import lax
from jax.experimental import pallas as pl
from jax.experimental.pallas import tpu as pltpu
from jax.sharding import PartitionSpec as P

F32 = jnp.float32
BF16 = jnp.bfloat16
MESH = pl.DeviceIdType.MESH
N = 4096
OWN, OPP = 16, 17


def two_parts(x):
    high = x.astype(ml_dtypes.bfloat16)
    low = (x - high.astype(np.float64)).astype(ml_dtypes.bfloat16)
    return np.stack([high, low])


def tables():
    k1 = np.arange(32)
    z, h = np.arange(16), np.arange(2)
    n1 = 16 * h[None, :] + z[:, None]
    angle = 2 * np.pi * ((k1[:, None, None] + 1) * n1[None] % 32) / 32
    first = np.stack([np.cos(angle), np.sin(angle)]) / math.sqrt(N)
    first = np.einsum("ckzh,pr->ckpzhr", first, np.eye(8)).reshape(512, 256)
    n2 = np.arange(128)
    angle = 2 * np.pi * ((k1[:, None] + 1) * n2[None] % N) / N
    twiddle = np.stack([np.cos(angle), np.sin(angle)])
    twiddle = np.repeat(twiddle, 8, axis=1).astype(np.float32)
    k2 = np.arange(32)
    angle = 2 * np.pi * (n2[:, None] * k2[None] % 128) / 128
    co, si = np.cos(angle), np.sin(angle)
    second = np.array([[co, si], [-si, co]])
    second = np.einsum("rcnk,ab->arncbk", second, np.eye(4)).reshape(1024, 256)
    k1b, k1a = np.arange(8), np.arange(4)
    k = 1 + 8 * k1a[None, :, None] + k1b[:, None, None] + 32 * k2[None, None, :]
    shift = np.arange(256) - 128
    angle = 2 * np.pi * (k.reshape(1024)[:, None] * shift[None] % N) / N
    lag = np.concatenate([np.cos(angle), -np.sin(angle)]).astype(ml_dtypes.bfloat16)
    return two_parts(first), twiddle, two_parts(second), lag


def kernel(
    series, assign, first_hbm, twiddle_hbm, second_hbm, lag_hbm,
    cross, opposite,
    first, twiddle, second, lag, send1, recv1, send2, recv2, units, wide, lhs,
    load_sem, send1_sem, recv1_sem, send2_sem, recv2_sem, sendu_sem, recvu_sem, sende_sem,
):
    me, q = lax.axis_index("blk"), lax.axis_index("pair")
    half, z, y = me // 64, me // 4 % 16, me % 4
    spot = half * 4 + y

    def device(blk, pair=None):
        return {"blk": blk, "pair": q if pair is None else pair}

    def peer1(s):
        return s // 4 * 64 + z * 4 + s % 4

    def peer2(zz):
        return half * 64 + zz * 4 + y

    barrier = pltpu.get_barrier_semaphore()

    def greet(blk, pair=None):
        pl.semaphore_signal(barrier, 1, device_id=device(blk, pair), device_id_type=MESH)

    low_pair = q < 2
    edge = jnp.where(low_pair, 0, 3)
    own_from = jnp.where(low_pair, me + 120, me + 72) % 128
    opp_from = jnp.where(low_pair, me + 56, me + 8) % 128
    for d in range(1, 8):
        greet(peer1((spot + d) % 8))
    for d in range(1, 16):
        greet(peer2((z + d) % 16))
    for m in range(16):
        if m != 8:
            greet((me + m + 120) % 128)
    greet(own_from, edge)
    greet(opp_from, edge)

    loads = [
        pltpu.make_async_copy(src, dst, load_sem.at[i])
        for i, (src, dst) in enumerate(
            [(first_hbm, first), (twiddle_hbm, twiddle), (second_hbm, second), (lag_hbm, lag)]
        )
    ]
    for c in loads:
        c.start()

    ids = assign[...]
    turned = pltpu.roll(ids, 64, 1)
    rows = [turned] + [pltpu.roll(turned, 8 - k, 0) for k in range(1, 5)]

    def pick(first_row):
        out = rows[first_row + 3]
        for k in (2, 1, 0):
            out = jnp.where(q == k, rows[first_row + k], out)
        return out

    lane = lax.broadcasted_iota(jnp.int32, (8, 128), 1)
    row = lax.broadcasted_iota(jnp.int32, (8, 128), 0)
    moved = jnp.where(lane < 64, pick(0), pick(1))
    wanted = {}
    for yy in range(4):
        index = lane // 8 % 4 * 32 + yy * 8 + lane % 8
        got = jnp.take_along_axis(moved, index, axis=1)
        got = jnp.where(lane // 32 == row % 4, got, 0)
        for hh in range(2):
            wanted[hh * 4 + yy] = jnp.sum(got[hh * 4 : hh * 4 + 4], axis=0, keepdims=True)

    probe = lax.broadcasted_iota(jnp.int32, (1024, 256), 0)
    for s in range(0, 8, 2):
        pair_ids = jnp.concatenate([wanted[s], wanted[s + 1]], axis=1)
        hot = jnp.where(probe == pair_ids, 1.0, 0.0).astype(BF16)
        part = jnp.dot(series[...], hot, preferred_element_type=F32).astype(BF16)
        send1[s] = part[:, :128]
        send1[s + 1] = part[:, 128:]

    pl.semaphore_wait(barrier, 7 + 15 + 15 + jnp.where(jnp.logical_or(q == 0, q == 3), 4, 0))

    def remote(src, dst, ssem, rsem, blk, pair=None):
        return pltpu.make_async_remote_copy(
            src_ref=src, dst_ref=dst, send_sem=ssem, recv_sem=rsem,
            device_id=device(blk, pair), device_id_type=MESH,
        )

    stage1 = []
    for d in range(1, 8):
        s = (spot + d) % 8
        stage1.append(remote(send1.at[s], recv1.at[spot], send1_sem.at[d], recv1_sem.at[d], peer1(s)))
        stage1[-1].start()
    recv1[spot] = send1[spot]
    for c in stage1:
        c.wait_recv()
    sides = []
    for hh in range(2):
        side = recv1[hh * 4 : hh * 4 + 4].reshape(128, 128).astype(F32)
        sides.append(jnp.transpose(side).reshape(16, 8, 128))
    send2[...] = jnp.concatenate(sides, axis=1).astype(BF16)

    stage2 = []
    for d in range(1, 16):
        zz = (z + d) % 16
        stage2.append(remote(send2.at[zz], recv2.at[z], send2_sem.at[d], recv2_sem.at[d], peer2(zz)))
        stage2[-1].start()
    recv2[z] = send2[z]
    loads[0].wait()
    loads[1].wait()
    loads[2].wait()
    for c in stage2:
        c.wait_recv()

    x = recv2[...].reshape(256, 128)
    a = jnp.dot(first[0], x, preferred_element_type=F32) + jnp.dot(first[1], x, preferred_element_type=F32)
    ac, as_ = a[:256], a[256:]
    tc, ts = twiddle[0], twiddle[1]
    bre, bim = ac * tc - as_ * ts, ac * ts + as_ * tc
    b = jnp.concatenate([v[64 * k : 64 * k + 64] for k in range(4) for v in (bre, bim)], axis=1)
    bhigh = b.astype(BF16)
    blow = (b - bhigh.astype(F32)).astype(BF16)
    spectrum = (
        jnp.dot(bhigh, second[0], preferred_element_type=F32)
        + jnp.dot(blow, second[0], preferred_element_type=F32)
        + jnp.dot(bhigh, second[1], preferred_element_type=F32)
    )
    re, im = spectrum[:, :128].reshape(8, 8, 128), spectrum[:, 128:].reshape(8, 8, 128)
    energy = jnp.sum(jnp.sum(re * re + im * im, axis=0), axis=1, keepdims=True)
    scale = lax.rsqrt(energy + 1e-06)
    for k in range(8):
        units[8, :, 128 * k : 128 * k + 128] = jnp.concatenate([re[k] * scale, im[k] * scale], axis=0).astype(BF16)

    mine = units.at[8]

    @pl.when(jnp.logical_or(q == 0, q == 3))
    def _():
        low = q == 0
        lane0 = jnp.where(low, 0, 2)
        own_to = jnp.where(low, me + 8, me + 56) % 128
        opp_to = jnp.where(low, me + 72, me + 120) % 128
        for k in range(2):
            remote(mine, units.at[OWN], sende_sem.at[k], recvu_sem.at[OWN], own_to, lane0 + k).start()
        for k in range(2):
            remote(mine, units.at[OPP], sende_sem.at[2 + k], recvu_sem.at[OPP], opp_to, lane0 + k).start()

    window = {}
    for m in (7, 9, 6, 10, 5, 11, 4, 12, 3, 13, 2, 14, 1, 15, 0):
        window[m] = remote(mine, units.at[m], sendu_sem.at[m], recvu_sem.at[m], (me + 136 - m) % 128)
        window[m].start()

    def arrived(slot):
        remote(mine, units.at[slot], sende_sem.at[0], recvu_sem.at[slot], own_from, edge).wait_recv()

    arrived(OWN)
    own = units[OWN].astype(F32)
    for i in range(8):
        for c in range(2):
            wide[c, i] = jnp.broadcast_to(own[8 * c + i : 8 * c + i + 1], (8, 1024))

    def products(slot):
        v = units[slot].astype(F32)
        v0, v1 = v[:8], v[8:]
        for i in range(0, 8, 2):
            real = [wide[0, i + j] * v0 + wide[1, i + j] * v1 for j in range(2)]
            imag = [wide[1, i + j] * v0 - wide[0, i + j] * v1 for j in range(2)]
            lhs[slot, 8 * i : 8 * i + 16, :1024] = jnp.concatenate(real, axis=0).astype(BF16)
            lhs[slot, 8 * i : 8 * i + 16, 1024:] = jnp.concatenate(imag, axis=0).astype(BF16)

    loads[3].wait()
    for chunk in (2, 1, 3, 0):
        for m in range(4 * chunk, 4 * chunk + 4):
            if m != 8:
                window[m].wait_recv()

        @pl.loop(4 * chunk, 4 * chunk + 4)
        def _(m):
            products(m)

        cross[256 * chunk : 256 * chunk + 256] = jnp.dot(
            lhs[4 * chunk : 4 * chunk + 4].reshape(256, 2048), lag[...], preferred_element_type=F32
        )
    arrived(OPP)
    products(OPP)
    far = jnp.dot(lhs[OPP], lag[...], preferred_element_type=F32)
    out = far[:, 192:]
    for k in range(3):
        out = jnp.where(q == k, far[:, 64 * k : 64 * k + 64], out)
    opposite[...] = out

    for c in stage1 + stage2 + list(window.values()):
        c.wait_send()

    @pl.when(jnp.logical_or(q == 0, q == 3))
    def _():
        for k in range(4):
            remote(mine, units.at[OWN], sende_sem.at[k], recvu_sem.at[OWN], own_from, edge).wait_send()


def body(series, assign):
    first, twiddle, second, lag = tables()
    vmem = pl.BlockSpec(memory_space=pltpu.VMEM)
    hbm = pl.BlockSpec(memory_space=pl.ANY)
    dma = pltpu.SemaphoreType.DMA
    cross, opposite = pl.pallas_call(
        kernel,
        out_shape=[jax.ShapeDtypeStruct((1024, 256), F32), jax.ShapeDtypeStruct((64, 64), F32)],
        in_specs=[vmem] * 2 + [hbm] * 4,
        out_specs=[vmem] * 2,
        scratch_shapes=[
            pltpu.VMEM(first.shape, BF16),
            pltpu.VMEM(twiddle.shape, F32),
            pltpu.VMEM(second.shape, BF16),
            pltpu.VMEM(lag.shape, BF16),
            pltpu.VMEM((8, 32, 128), BF16),
            pltpu.VMEM((8, 32, 128), BF16),
            pltpu.VMEM((16, 16, 128), BF16),
            pltpu.VMEM((16, 16, 128), BF16),
            pltpu.VMEM((18, 16, 1024), BF16),
            pltpu.VMEM((2, 8, 8, 1024), F32),
            pltpu.VMEM((18, 64, 2048), BF16),
            dma((4,)), dma((8,)), dma((8,)), dma((16,)), dma((16,)), dma((16,)), dma((18,)), dma((4,)),
        ],
        compiler_params=pltpu.CompilerParams(
            collective_id=0, has_side_effects=True, vmem_limit_bytes=40 * 1024 * 1024
        ),
    )(series.T, assign.reshape(8, 128), first, twiddle, second, lag)
    return cross.reshape(1, 1, 16, 8, 8, 256), opposite.reshape(1, 8, 8, 64)


def solution(mesh):
    in_specs = (P(None, "blk"), P())
    out_specs = (P("blk", "pair", None, None, None, None), P("blk", None, None, "pair"))
    return jax.shard_map(body, mesh=mesh, in_specs=in_specs, out_specs=out_specs, check_vma=False)
```

```python
import math

import jax
import jax.numpy as jnp
import ml_dtypes
import numpy as np
from jax import lax
from jax.experimental import pallas as pl
from jax.experimental.pallas import tpu as pltpu
from jax.sharding import PartitionSpec as P

F32 = jnp.float32
BF16 = jnp.bfloat16
MESH = pl.DeviceIdType.MESH
N = 4096
PASS, OWN, OPP = 16, 17, 18


def two_parts(x):
    high = x.astype(ml_dtypes.bfloat16)
    low = (x - high.astype(np.float64)).astype(ml_dtypes.bfloat16)
    return np.stack([high, low])


def tables():
    k1 = np.arange(32)
    z, h = np.arange(16), np.arange(2)
    n1 = 16 * h[None, :] + z[:, None]
    angle = 2 * np.pi * ((k1[:, None, None] + 1) * n1[None] % 32) / 32
    first = np.stack([np.cos(angle), np.sin(angle)]) / math.sqrt(N)
    first = np.einsum("ckzh,pr->ckpzhr", first, np.eye(8)).reshape(512, 256)
    n2 = np.arange(128)
    angle = 2 * np.pi * ((k1[:, None] + 1) * n2[None] % N) / N
    twiddle = np.stack([np.cos(angle), np.sin(angle)])
    twiddle = np.repeat(twiddle, 8, axis=1).astype(np.float32)
    k2 = np.arange(32)
    angle = 2 * np.pi * (n2[:, None] * k2[None] % 128) / 128
    co, si = np.cos(angle), np.sin(angle)
    second = np.array([[co, si], [-si, co]])
    second = np.einsum("rcnk,ab->arncbk", second, np.eye(4)).reshape(1024, 256)
    k1b, k1a = np.arange(8), np.arange(4)
    k = 1 + 8 * k1a[None, :, None] + k1b[:, None, None] + 32 * k2[None, None, :]
    shift = np.arange(256) - 128
    angle = 2 * np.pi * (k.reshape(1024)[:, None] * shift[None] % N) / N
    lag = np.concatenate([np.cos(angle), -np.sin(angle)]).astype(ml_dtypes.bfloat16)
    return two_parts(first), twiddle, two_parts(second), lag


def kernel(
    series_hbm, assign_hbm, first_hbm, twiddle_hbm, second_hbm, lag_hbm,
    cross, opposite,
    series, assign, first, twiddle, second, lag, send1, recv1, send2, recv2, units, wide, lhs,
    load_sem, send1_sem, recv1_sem, send2_sem, recv2_sem, sendu_sem, recvu_sem, near_sem, far_sem,
):
    me, q = lax.axis_index("blk"), lax.axis_index("pair")
    half, z, y = me // 64, me // 4 % 16, me % 4
    spot = half * 4 + y

    def device(blk, pair=None):
        return {"blk": blk, "pair": q if pair is None else pair}

    def peer1(s):
        return s // 4 * 64 + z * 4 + s % 4

    def peer2(zz):
        return half * 64 + zz * 4 + y

    loads = [
        pltpu.make_async_copy(src, dst, load_sem.at[i])
        for i, (src, dst) in enumerate(
            [(first_hbm, first), (twiddle_hbm, twiddle), (second_hbm, second), (lag_hbm, lag),
             (assign_hbm, assign), (series_hbm, series)]
        )
    ]
    for c in loads[::-1]:
        c.start()

    barrier = pltpu.get_barrier_semaphore()
    core = q % 2
    other = q + 1 - 2 * core

    def greet(blk, pair):
        pl.semaphore_signal(barrier, 1, device_id=device(blk, pair), device_id_type=MESH)

    greet(me, other)
    for d in range(1, 8):
        greet(peer1((spot + d) % 8), q - core + 1)
    for d in range(1, 16):
        greet(peer2((z + d) % 16), q - core)
    for d in (4, 8, 120, 124):
        greet((me + d) % 128, q - core)

    @pl.when(q >= 2)
    def _():
        greet(me, 0)
        greet((me + 64) % 128, 0)

    @pl.when(core == 1)
    def _():
        pl.semaphore_wait(barrier, 1 + 2 * 7)
        pl.semaphore_signal(near_sem, 1, device_id=device(me, other), device_id_type=MESH)

    loads[4].wait()
    ids = assign[...]
    turned = pltpu.roll(ids, 64, 1)
    rows = [turned] + [pltpu.roll(turned, 8 - k, 0) for k in range(1, 5)]

    def pick(first_row):
        out = rows[first_row + 3]
        for k in (2, 1, 0):
            out = jnp.where(q == k, rows[first_row + k], out)
        return out

    lane = lax.broadcasted_iota(jnp.int32, (8, 128), 1)
    row = lax.broadcasted_iota(jnp.int32, (8, 128), 0)
    moved = jnp.where(lane < 64, pick(0), pick(1))
    wanted = {}
    for yy in range(4):
        index = lane // 8 % 4 * 32 + yy * 8 + lane % 8
        got = jnp.take_along_axis(moved, index, axis=1)
        got = jnp.where(lane // 32 == row % 4, got, 0)
        for hh in range(2):
            wanted[hh * 4 + yy] = jnp.sum(got[hh * 4 : hh * 4 + 4], axis=0, keepdims=True)

    loads[5].wait()
    samples = series[...].astype(F32)
    for s in range(8):
        ids = jnp.broadcast_to(wanted[s], (32, 128))
        source, index = ids // 128, ids % 128
        part = jnp.zeros((32, 128), F32)
        for k in range(8):
            got = jnp.take_along_axis(samples[:, 128 * k : 128 * k + 128], index, axis=1)
            part = jnp.where(source == k, got, part)
        send1[s] = part.astype(BF16)

    @pl.when(core == 0)
    def _():
        pl.semaphore_wait(near_sem, 1)

    def remote(src, dst, ssem, rsem, blk, pair=None):
        return pltpu.make_async_remote_copy(
            src_ref=src, dst_ref=dst, send_sem=ssem, recv_sem=rsem,
            device_id=device(blk, pair), device_id_type=MESH,
        )

    stage1 = []
    for d in (6, 5, 7, 2, 4, 1, 3):
        s = (spot + d) % 8
        stage1.append(remote(send1.at[s], recv1.at[spot], send1_sem.at[d], recv1_sem.at[d], peer1(s)))
        stage1[-1].start()
    recv1[spot] = send1[spot]

    @pl.when(core == 0)
    def _():
        pl.semaphore_wait(barrier, 1 + 2 * (15 + 4) + jnp.where(q == 0, 4, 0))
        pl.semaphore_signal(far_sem, 1, device_id=device(me, other), device_id_type=MESH)

    for c in stage1:
        c.wait_recv()
    sides = []
    for hh in range(2):
        side = recv1[hh * 4 : hh * 4 + 4].reshape(128, 128).astype(F32)
        sides.append(jnp.transpose(side).reshape(16, 8, 128))
    send2[...] = jnp.concatenate(sides, axis=1).astype(BF16)

    @pl.when(core == 1)
    def _():
        pl.semaphore_wait(far_sem, 1)

    stage2 = []
    for d in (8, 7, 9, 6, 10, 5, 11, 4, 12, 3, 13, 2, 14, 1, 15):
        zz = (z + d) % 16
        stage2.append(remote(send2.at[zz], recv2.at[z], send2_sem.at[d], recv2_sem.at[d], peer2(zz)))
        stage2[-1].start()
    recv2[z] = send2[z]
    loads[0].wait()
    loads[1].wait()
    loads[2].wait()
    for c in stage2:
        c.wait_recv()

    x = recv2[...].reshape(256, 128)
    a = jnp.dot(first[0], x, preferred_element_type=F32) + jnp.dot(first[1], x, preferred_element_type=F32)
    ac, as_ = a[:256], a[256:]
    tc, ts = twiddle[0], twiddle[1]
    bre, bim = ac * tc - as_ * ts, ac * ts + as_ * tc
    b = jnp.concatenate([v[64 * k : 64 * k + 64] for k in range(4) for v in (bre, bim)], axis=1)
    bhigh = b.astype(BF16)
    blow = (b - bhigh.astype(F32)).astype(BF16)
    spectrum = (
        jnp.dot(bhigh, second[0], preferred_element_type=F32)
        + jnp.dot(blow, second[0], preferred_element_type=F32)
        + jnp.dot(bhigh, second[1], preferred_element_type=F32)
    )
    re, im = spectrum[:, :128].reshape(8, 8, 128), spectrum[:, 128:].reshape(8, 8, 128)
    energy = jnp.sum(jnp.sum(re * re + im * im, axis=0), axis=1, keepdims=True)
    scale = lax.rsqrt(energy + 1e-06)
    for k in range(8):
        units[8 + y, :, 128 * k : 128 * k + 128] = jnp.concatenate([re[k] * scale, im[k] * scale], axis=0).astype(BF16)

    mine = units.at[8 + y]
    sent = []

    def send(src, slot, blk, pair=None):
        sem = sendu_sem.at[len(sent)]
        sent.append(remote(src, units.at[slot], sem, recvu_sem.at[slot], blk, pair))
        return sent[-1]

    def arrived(slot):
        remote(mine, units.at[slot], sendu_sem.at[0], recvu_sem.at[slot], (me + 4) % 128).wait_recv()

    up2, down2 = (me + 8) % 128, (me + 120) % 128
    up1, down1 = (me + 4) % 128, (me + 124) % 128
    column = {k: (y + k) % 4 for k in (1, 2, 3)}
    slab = me // 4 * 4
    to_up2 = send(mine, y, up2)
    to_down2 = send(mine, PASS, down2)
    to_up2.start()
    send(mine, 8 + y, slab + column[2]).start()

    @pl.when(y < 3)
    def _():
        to_down2.start()

    send(mine, 8 + y, slab + column[1]).start()
    send(mine, 8 + y, slab + column[3]).start()
    send(mine, 4 + y, up1).start()
    send(mine, 12 + y, down1).start()
    for k in (1, 3):
        arrived(8 + column[k])
        send(units.at[8 + column[k]], 4 + column[k], up1).start()
        send(units.at[8 + column[k]], 12 + column[k], down1).start()
    arrived(y)
    extras = [send(units.at[y], OWN, me, lane) for lane in (2, 3, 1)]
    extras += [send(units.at[y], OPP, (me + 64) % 128, lane) for lane in (2, 3, 0, 1)]

    @pl.when(q == 0)
    def _():
        for c in extras:
            c.start()

    @pl.when(y < 3)
    def _():
        arrived(PASS)

    for k in (2, 1, 3):
        send(units.at[jnp.where(column[k] < y, y, PASS)], y, slab + column[k]).start()
    arrived(8 + column[2])
    send(units.at[8 + column[2]], 4 + column[2], up1).start()
    send(units.at[8 + column[2]], 12 + column[2], down1).start()

    @pl.when(q > 0)
    def _():
        arrived(OWN)

    own = units[jnp.where(q == 0, y, OWN)].astype(F32)
    for i in range(8):
        for c in range(2):
            wide[c, i] = jnp.broadcast_to(own[8 * c + i : 8 * c + i + 1], (8, 1024))

    def products(slot):
        v = units[slot].astype(F32)
        v0, v1 = v[:8], v[8:]
        for i in range(0, 8, 2):
            real = [wide[0, i + j] * v0 + wide[1, i + j] * v1 for j in range(2)]
            imag = [wide[1, i + j] * v0 - wide[0, i + j] * v1 for j in range(2)]
            lhs[slot, 8 * i : 8 * i + 16, :1024] = jnp.concatenate(real, axis=0).astype(BF16)
            lhs[slot, 8 * i : 8 * i + 16, 1024:] = jnp.concatenate(imag, axis=0).astype(BF16)

    loads[3].wait()

    def chunk(first_slot):
        for slot in range(first_slot, first_slot + 4):
            products(slot)
        rows = lhs[first_slot : first_slot + 4].reshape(256, 2048)
        return jnp.dot(rows, lag[...], preferred_element_type=F32).reshape(4, 64, 256)

    cross[pl.ds(8 - y, 4)] = chunk(8)
    for first_slot in (4, 12):
        for k in range(4):
            arrived(first_slot + k)
        cross[pl.ds(first_slot - y, 4)] = chunk(first_slot)
    arrived(OPP)
    products(OPP)
    far = jnp.dot(lhs[OPP], lag[...], preferred_element_type=F32)
    out = far[:, 192:]
    for k in range(3):
        out = jnp.where(q == k, far[:, 64 * k : 64 * k + 64], out)
    opposite[...] = out
    for k in (1, 2, 3):
        arrived(column[k])
    ends = chunk(0)
    for k in range(4):
        cross[(k - y + 16) % 16] = ends[k]

    for c in stage1 + stage2:
        c.wait_send()
    special = [id(c) for c in [to_down2] + extras]
    for c in sent:
        if id(c) not in special:
            c.wait_send()

    @pl.when(y < 3)
    def _():
        to_down2.wait_send()

    @pl.when(q == 0)
    def _():
        for c in extras:
            c.wait_send()


def finish(cross, opposite, cross_out, opposite_out, sem):
    copies = [
        pltpu.make_async_copy(cross, cross_out, sem.at[0]),
        pltpu.make_async_copy(opposite, opposite_out, sem.at[1]),
    ]
    for c in copies:
        c.start()
    for c in copies:
        c.wait()


def body(series, assign):
    first, twiddle, second, lag = tables()
    vmem = pl.BlockSpec(memory_space=pltpu.VMEM)
    hbm = pl.BlockSpec(memory_space=pltpu.HBM)
    dma = pltpu.SemaphoreType.DMA
    cross, opposite = pl.pallas_call(
        kernel,
        out_shape=[pltpu.VMEM((16, 64, 256), F32), pltpu.VMEM((64, 64), F32)],
        in_specs=[hbm] * 6,
        out_specs=[vmem] * 2,
        scratch_shapes=[
            pltpu.VMEM((32, 1024), BF16),
            pltpu.VMEM((8, 128), jnp.int32),
            pltpu.VMEM(first.shape, BF16),
            pltpu.VMEM(twiddle.shape, F32),
            pltpu.VMEM(second.shape, BF16),
            pltpu.VMEM(lag.shape, BF16),
            pltpu.VMEM((8, 32, 128), BF16),
            pltpu.VMEM((8, 32, 128), BF16),
            pltpu.VMEM((16, 16, 128), BF16),
            pltpu.VMEM((16, 16, 128), BF16),
            pltpu.VMEM((19, 16, 1024), BF16),
            pltpu.VMEM((2, 8, 8, 1024), F32),
            pltpu.VMEM((19, 64, 2048), BF16),
            dma((6,)), dma((8,)), dma((8,)), dma((16,)), dma((16,)), dma((23,)), dma((19,)),
            pltpu.SemaphoreType.REGULAR, pltpu.SemaphoreType.REGULAR,
        ],
        compiler_params=pltpu.CompilerParams(
            collective_id=0, has_side_effects=True, vmem_limit_bytes=60 * 1024 * 1024
        ),
    )(series.T, assign.reshape(8, 128), first, twiddle, second, lag)
    cross, opposite = pl.pallas_call(
        finish,
        out_shape=[jax.ShapeDtypeStruct((16, 64, 256), F32), jax.ShapeDtypeStruct((64, 64), F32)],
        in_specs=[vmem] * 2,
        out_specs=[pl.BlockSpec(memory_space=pltpu.HBM)] * 2,
        scratch_shapes=[dma((2,))],
        compiler_params=pltpu.CompilerParams(vmem_limit_bytes=2 * 1024 * 1024),
    )(cross, opposite)
    return cross.reshape(1, 1, 16, 8, 8, 256), opposite.reshape(1, 8, 8, 64)


def solution(mesh):
    in_specs = (P(None, "blk"), P())
    out_specs = (P("blk", "pair", None, None, None, None), P("blk", None, None, "pair"))
    return jax.shard_map(body, mesh=mesh, in_specs=in_specs, out_specs=out_specs, check_vma=False)
```

```python
import math

import jax
import jax.numpy as jnp
import ml_dtypes
import numpy as np
from jax import lax
from jax.experimental import pallas as pl
from jax.experimental.pallas import tpu as pltpu
from jax.sharding import PartitionSpec as P

F32 = jnp.float32
BF16 = jnp.bfloat16
MESH = pl.DeviceIdType.MESH
N = 4096
PASS, OWN, OPP = 16, 17, 18


def two_parts(x):
    high = x.astype(ml_dtypes.bfloat16)
    low = (x - high.astype(np.float64)).astype(ml_dtypes.bfloat16)
    return np.stack([high, low])


def tables():
    k1 = np.arange(32)
    z, h = np.arange(16), np.arange(2)
    n1 = 16 * h[None, :] + z[:, None]
    angle = 2 * np.pi * ((k1[:, None, None] + 1) * n1[None] % 32) / 32
    first = np.stack([np.cos(angle), np.sin(angle)]) / math.sqrt(N)
    first = np.einsum("ckzh,pr->ckpzhr", first, np.eye(8)).reshape(512, 256)
    n2 = np.arange(128)
    angle = 2 * np.pi * ((k1[:, None] + 1) * n2[None] % N) / N
    twiddle = np.stack([np.cos(angle), np.sin(angle)])
    twiddle = np.repeat(twiddle, 8, axis=1).astype(np.float32)
    k2 = np.arange(32)
    angle = 2 * np.pi * (n2[:, None] * k2[None] % 128) / 128
    co, si = np.cos(angle), np.sin(angle)
    second = np.array([[co, si], [-si, co]])
    second = np.einsum("rcnk,ab->arncbk", second, np.eye(4)).reshape(1024, 256)
    k1b, k1a = np.arange(8), np.arange(4)
    k = 1 + 8 * k1a[None, :, None] + k1b[:, None, None] + 32 * k2[None, None, :]
    shift = np.arange(256) - 128
    angle = 2 * np.pi * (k.reshape(1024)[:, None] * shift[None] % N) / N
    lag = np.concatenate([np.cos(angle), -np.sin(angle)]).astype(ml_dtypes.bfloat16)
    return two_parts(first), twiddle, two_parts(second), lag


def kernel(
    series_hbm, assign_hbm, first_hbm, twiddle_hbm, second_hbm, lag_hbm,
    cross, opposite,
    series, assign, first, twiddle, second, lag, send1, recv1, send2, recv2, units, wide, lhs,
    load_sem, send1_sem, recv1_sem, send2_sem, recv2_sem, sendu_sem, recvu_sem, near_sem, far_sem,
):
    me, q = lax.axis_index("blk"), lax.axis_index("pair")
    half, z, y = me // 64, me // 4 % 16, me % 4
    spot = half * 4 + y

    def device(blk, pair=None):
        return {"blk": blk, "pair": q if pair is None else pair}

    def peer1(s):
        return s // 4 * 64 + z * 4 + s % 4

    def peer2(zz):
        return half * 64 + zz * 4 + y

    loads = [
        pltpu.make_async_copy(src, dst, load_sem.at[i])
        for i, (src, dst) in enumerate(
            [(first_hbm, first), (twiddle_hbm, twiddle), (second_hbm, second), (lag_hbm, lag),
             (assign_hbm, assign), (series_hbm, series)]
        )
    ]
    for c in loads[::-1]:
        c.start()

    barrier = pltpu.get_barrier_semaphore()
    core = q % 2
    other = q + 1 - 2 * core

    def greet(blk, pair):
        pl.semaphore_signal(barrier, 1, device_id=device(blk, pair), device_id_type=MESH)

    slab = me // 4 * 4
    up1, down1, up2, down2 = (slab + 4) % 128, (slab + 124) % 128, (slab + 8) % 128, (slab + 120) % 128
    column = {k: (y + k) % 4 for k in (1, 2, 3)}
    greet(me, other)
    for d in (8, 7, 9, 6, 10, 5, 11, 4, 12, 3, 13, 2, 14, 1, 15):
        greet(peer2((z + d) % 16), q - core)
    for d in range(1, 8):
        greet(peer1((spot + d) % 8), q - core + 1)
    for blk in (up1, down1, up2, down2):
        greet(blk + y, q - core)
    for blk in (up1, down1):
        for k in (1, 3):
            greet(blk + column[k], q - core)

    @pl.when(q >= 2)
    def _():
        greet((me + 72) % 128, 2)

    @pl.when(core == 1)
    def _():
        pl.semaphore_wait(barrier, 1 + 2 * 7)
        pl.semaphore_signal(near_sem, 1, device_id=device(me, other), device_id_type=MESH)

    loads[4].wait()
    ids = assign[...]
    turned = pltpu.roll(ids, 64, 1)
    rows = [turned] + [pltpu.roll(turned, 8 - k, 0) for k in range(1, 5)]

    def pick(first_row):
        out = rows[first_row + 3]
        for k in (2, 1, 0):
            out = jnp.where(q == k, rows[first_row + k], out)
        return out

    lane = lax.broadcasted_iota(jnp.int32, (8, 128), 1)
    row = lax.broadcasted_iota(jnp.int32, (8, 128), 0)
    moved = jnp.where(lane < 64, pick(0), pick(1))
    wanted = {}
    for yy in range(4):
        index = lane // 8 % 4 * 32 + yy * 8 + lane % 8
        got = jnp.take_along_axis(moved, index, axis=1)
        got = jnp.where(lane // 32 == row % 4, got, 0)
        for hh in range(2):
            wanted[hh * 4 + yy] = jnp.sum(got[hh * 4 : hh * 4 + 4], axis=0, keepdims=True)

    loads[5].wait()
    samples = series[...].astype(F32)
    for s in range(8):
        ids = jnp.broadcast_to(wanted[s], (32, 128))
        source, index = ids // 128, ids % 128
        part = jnp.zeros((32, 128), F32)
        for k in range(8):
            got = jnp.take_along_axis(samples[:, 128 * k : 128 * k + 128], index, axis=1)
            part = jnp.where(source == k, got, part)
        send1[s] = part.astype(BF16)

    @pl.when(core == 0)
    def _():
        pl.semaphore_wait(near_sem, 1)

    def remote(src, dst, ssem, rsem, blk, pair=None):
        return pltpu.make_async_remote_copy(
            src_ref=src, dst_ref=dst, send_sem=ssem, recv_sem=rsem,
            device_id=device(blk, pair), device_id_type=MESH,
        )

    stage1 = []
    for d in (6, 5, 7, 2, 4, 1, 3):
        s = (spot + d) % 8
        stage1.append(remote(send1.at[s], recv1.at[spot], send1_sem.at[d], recv1_sem.at[d], peer1(s)))
        stage1[-1].start()
    recv1[spot] = send1[spot]

    @pl.when(core == 0)
    def _():
        pl.semaphore_wait(barrier, 1 + 2 * (15 + 4 + 4) + jnp.where(q == 2, 2, 0))
        pl.semaphore_signal(far_sem, 1, device_id=device(me, other), device_id_type=MESH)

    for c in stage1:
        c.wait_recv()
    sides = []
    for hh in range(2):
        side = recv1[hh * 4 : hh * 4 + 4].reshape(128, 128).astype(F32)
        sides.append(jnp.transpose(side).reshape(16, 8, 128))
    send2[...] = jnp.concatenate(sides, axis=1).astype(BF16)

    @pl.when(core == 1)
    def _():
        pl.semaphore_wait(far_sem, 1)

    stage2 = []
    for d in (8, 7, 9, 6, 10, 5, 11, 4, 12, 3, 13, 2, 14, 1, 15):
        zz = (z + d) % 16
        stage2.append(remote(send2.at[zz], recv2.at[z], send2_sem.at[d], recv2_sem.at[d], peer2(zz)))
        stage2[-1].start()
    recv2[z] = send2[z]
    loads[0].wait()
    loads[1].wait()
    loads[2].wait()
    for c in stage2:
        c.wait_recv()

    x = recv2[...].reshape(256, 128)
    a = jnp.dot(first[0], x, preferred_element_type=F32) + jnp.dot(first[1], x, preferred_element_type=F32)
    ac, as_ = a[:256], a[256:]
    tc, ts = twiddle[0], twiddle[1]
    bre, bim = ac * tc - as_ * ts, ac * ts + as_ * tc
    b = jnp.concatenate([v[64 * k : 64 * k + 64] for k in range(4) for v in (bre, bim)], axis=1)
    bhigh = b.astype(BF16)
    blow = (b - bhigh.astype(F32)).astype(BF16)
    spectrum = (
        jnp.dot(bhigh, second[0], preferred_element_type=F32)
        + jnp.dot(blow, second[0], preferred_element_type=F32)
        + jnp.dot(bhigh, second[1], preferred_element_type=F32)
    )
    re, im = spectrum[:, :128].reshape(8, 8, 128), spectrum[:, 128:].reshape(8, 8, 128)
    energy = jnp.sum(jnp.sum(re * re + im * im, axis=0), axis=1, keepdims=True)
    scale = lax.rsqrt(energy + 1e-06)
    for k in range(8):
        units[8 + y, :, 128 * k : 128 * k + 128] = jnp.concatenate([re[k] * scale, im[k] * scale], axis=0).astype(BF16)

    mine = units.at[8 + y]
    sent = []

    def send(src, slot, blk, pair=None):
        sem = sendu_sem.at[len(sent)]
        sent.append(remote(src, units.at[slot], sem, recvu_sem.at[slot], blk, pair))
        return sent[-1]

    def arrived(slot):
        remote(mine, units.at[slot], sendu_sem.at[0], recvu_sem.at[slot], (me + 4) % 128).wait_recv()

    to_up2 = send(mine, y, up2 + y)
    to_own = [send(mine, OWN, up2 + y, 1)] + [send(mine, OWN, (me + 56) % 128, lane) for lane in (2, 3)]
    to_down2 = send(mine, PASS, down2 + y)
    to_up2.start()

    @pl.when(q == 0)
    def _():
        to_own[0].start()

    @pl.when(q == 3)
    def _():
        to_own[1].start()
        to_own[2].start()

    send(mine, 8 + y, slab + column[2]).start()

    @pl.when(y < 3)
    def _():
        to_down2.start()

    for k in (1, 3):
        send(mine, 8 + y, slab + column[k]).start()
    send(mine, 4 + y, up1 + y).start()
    send(mine, 12 + y, down1 + y).start()
    for k in (1, 3):
        send(mine, 4 + y, up1 + column[k]).start()
        send(mine, 12 + y, down1 + column[k]).start()

    arrived(8 + column[2])
    send(units.at[8 + column[2]], 4 + column[2], up1 + y).start()
    send(units.at[8 + column[2]], 12 + column[2], down1 + y).start()
    arrived(y)

    @pl.when(y < 3)
    def _():
        arrived(PASS)

    for k in (2, 1, 3):
        send(units.at[jnp.where(column[k] < y, y, PASS)], y, slab + column[k]).start()

    @pl.when(q > 0)
    def _():
        arrived(OWN)

    own_slot = jnp.where(q == 0, y, OWN)
    send(units.at[own_slot], OPP, (me + 64) % 128).start()
    own = units[own_slot].astype(F32)
    for i in range(8):
        for c in range(2):
            wide[c, i] = jnp.broadcast_to(own[8 * c + i : 8 * c + i + 1], (8, 1024))

    def products(slot, spot):
        v = units[slot].astype(F32)
        v0, v1 = v[:8], v[8:]
        for i in range(0, 8, 2):
            real = [wide[0, i + j] * v0 + wide[1, i + j] * v1 for j in range(2)]
            imag = [wide[1, i + j] * v0 - wide[0, i + j] * v1 for j in range(2)]
            lhs[spot, 8 * i : 8 * i + 16, :1024] = jnp.concatenate(real, axis=0).astype(BF16)
            lhs[spot, 8 * i : 8 * i + 16, 1024:] = jnp.concatenate(imag, axis=0).astype(BF16)

    def correlate(first_spot, slots):
        for k, slot in enumerate(slots):
            products(slot, first_spot + k)
        rows = lhs[first_spot : first_spot + len(slots)].reshape(64 * len(slots), 2048)
        out = jnp.dot(rows, lag[...], preferred_element_type=F32)
        for k, slot in enumerate(slots):
            if not isinstance(slot, int) or slot != OPP:
                cross[(slot - y + 16) % 16] = out[64 * k : 64 * k + 64]
        return out

    loads[3].wait()
    arrived(8 + column[1])
    arrived(8 + column[3])
    correlate(0, [8, 9, 10, 11])
    near = [first + c for first in (4, 12) for c in (y, column[1], column[3])]
    for slot in near:
        arrived(slot)
    correlate(4, [y] + near)
    late = [4 + column[2], 12 + column[2]]
    for slot in late + [OPP]:
        arrived(slot)
    far = correlate(11, late + [OPP])[128:]
    out = far[:, 192:]
    for k in range(3):
        out = jnp.where(q == k, far[:, 64 * k : 64 * k + 64], out)
    opposite[...] = out
    edges = [column[k] for k in (1, 2, 3)]
    for slot in edges:
        arrived(slot)
    correlate(14, edges)

    for c in stage1 + stage2:
        c.wait_send()
    special = [id(c) for c in [to_down2] + to_own]
    for c in sent:
        if id(c) not in special:
            c.wait_send()

    @pl.when(y < 3)
    def _():
        to_down2.wait_send()

    @pl.when(q == 0)
    def _():
        to_own[0].wait_send()

    @pl.when(q == 3)
    def _():
        to_own[1].wait_send()
        to_own[2].wait_send()


def finish(cross, opposite, cross_out, opposite_out, sem):
    copies = [
        pltpu.make_async_copy(cross, cross_out, sem.at[0]),
        pltpu.make_async_copy(opposite, opposite_out, sem.at[1]),
    ]
    for c in copies:
        c.start()
    for c in copies:
        c.wait()


def body(series, assign):
    first, twiddle, second, lag = tables()
    vmem = pl.BlockSpec(memory_space=pltpu.VMEM)
    hbm = pl.BlockSpec(memory_space=pltpu.HBM)
    dma = pltpu.SemaphoreType.DMA
    cross, opposite = pl.pallas_call(
        kernel,
        out_shape=[pltpu.VMEM((16, 64, 256), F32), pltpu.VMEM((64, 64), F32)],
        in_specs=[hbm] * 6,
        out_specs=[vmem] * 2,
        scratch_shapes=[
            pltpu.VMEM((32, 1024), BF16),
            pltpu.VMEM((8, 128), jnp.int32),
            pltpu.VMEM(first.shape, BF16),
            pltpu.VMEM(twiddle.shape, F32),
            pltpu.VMEM(second.shape, BF16),
            pltpu.VMEM(lag.shape, BF16),
            pltpu.VMEM((8, 32, 128), BF16),
            pltpu.VMEM((8, 32, 128), BF16),
            pltpu.VMEM((16, 16, 128), BF16),
            pltpu.VMEM((16, 16, 128), BF16),
            pltpu.VMEM((19, 16, 1024), BF16),
            pltpu.VMEM((2, 8, 8, 1024), F32),
            pltpu.VMEM((17, 64, 2048), BF16),
            dma((6,)), dma((8,)), dma((8,)), dma((16,)), dma((16,)), dma((23,)), dma((19,)),
            pltpu.SemaphoreType.REGULAR, pltpu.SemaphoreType.REGULAR,
        ],
        compiler_params=pltpu.CompilerParams(
            collective_id=0, has_side_effects=True, vmem_limit_bytes=60 * 1024 * 1024
        ),
    )(series.T, assign.reshape(8, 128), first, twiddle, second, lag)
    cross, opposite = pl.pallas_call(
        finish,
        out_shape=[jax.ShapeDtypeStruct((16, 64, 256), F32), jax.ShapeDtypeStruct((64, 64), F32)],
        in_specs=[vmem] * 2,
        out_specs=[pl.BlockSpec(memory_space=pltpu.HBM)] * 2,
        scratch_shapes=[dma((2,))],
        compiler_params=pltpu.CompilerParams(vmem_limit_bytes=2 * 1024 * 1024),
    )(cross, opposite)
    return cross.reshape(1, 1, 16, 8, 8, 256), opposite.reshape(1, 8, 8, 64)


def solution(mesh):
    in_specs = (P(None, "blk"), P())
    out_specs = (P("blk", "pair", None, None, None, None), P("blk", None, None, "pair"))
    return jax.shard_map(body, mesh=mesh, in_specs=in_specs, out_specs=out_specs, check_vma=False)
```

```python
import math

import jax
import jax.numpy as jnp
import ml_dtypes
import numpy as np
from jax import lax
from jax.experimental import pallas as pl
from jax.experimental.pallas import tpu as pltpu
from jax.sharding import PartitionSpec as P

F32 = jnp.float32
BF16 = jnp.bfloat16
MESH = pl.DeviceIdType.MESH
N = 4096
PASS, OWN, OPP = 16, 17, 18


def two_parts(x):
    high = x.astype(ml_dtypes.bfloat16)
    low = (x - high.astype(np.float64)).astype(ml_dtypes.bfloat16)
    return np.stack([high, low])


def tables():
    k1 = np.arange(32)
    z, h = np.arange(16), np.arange(2)
    n1 = 16 * h[None, :] + z[:, None]
    angle = 2 * np.pi * ((k1[:, None, None] + 1) * n1[None] % 32) / 32
    first = np.stack([np.cos(angle), np.sin(angle)]) / math.sqrt(N)
    first = np.einsum("ckzh,pr->ckpzhr", first, np.eye(8)).reshape(512, 256)
    n2 = np.arange(128)
    angle = 2 * np.pi * ((k1[:, None] + 1) * n2[None] % N) / N
    twiddle = np.stack([np.cos(angle), np.sin(angle)])
    twiddle = np.repeat(twiddle, 8, axis=1).astype(np.float32)
    k2 = np.arange(32)
    angle = 2 * np.pi * (n2[:, None] * k2[None] % 128) / 128
    co, si = np.cos(angle), np.sin(angle)
    second = np.array([[co, si], [-si, co]])
    second = np.einsum("rcnk,ab->arncbk", second, np.eye(4)).reshape(1024, 256)
    k1b, k1a = np.arange(8), np.arange(4)
    k = 1 + 8 * k1a[None, :, None] + k1b[:, None, None] + 32 * k2[None, None, :]
    shift = np.arange(256) - 128
    angle = 2 * np.pi * (k.reshape(1024)[:, None] * shift[None] % N) / N
    lag = np.concatenate([np.cos(angle), -np.sin(angle)]).astype(ml_dtypes.bfloat16)
    return two_parts(first), twiddle, two_parts(second), lag


def kernel(
    series_hbm, assign_hbm, first_hbm, twiddle_hbm, second_hbm, lag_hbm,
    cross, opposite,
    series, assign, first, twiddle, second, lag, send1, recv1, send2, recv2, units, wide, lhs,
    load_sem, send1_sem, recv1_sem, send2_sem, recv2_sem, sendu_sem, recvu_sem, near_sem, far_sem,
):
    me, q = lax.axis_index("blk"), lax.axis_index("pair")
    half, z, y = me // 64, me // 4 % 16, me % 4
    spot = half * 4 + y

    def device(blk, pair=None):
        return {"blk": blk, "pair": q if pair is None else pair}

    def peer1(s):
        return s // 4 * 64 + z * 4 + s % 4

    def peer2(zz):
        return half * 64 + zz * 4 + y

    loads = [
        pltpu.make_async_copy(src, dst, load_sem.at[i])
        for i, (src, dst) in enumerate(
            [(first_hbm, first), (twiddle_hbm, twiddle), (second_hbm, second), (lag_hbm, lag),
             (assign_hbm, assign), (series_hbm, series)]
        )
    ]
    for c in loads[4:]:
        c.start()

    barrier = pltpu.get_barrier_semaphore()
    core = q % 2
    other = q + 1 - 2 * core

    def greet(blk, pair):
        pl.semaphore_signal(barrier, 1, device_id=device(blk, pair), device_id_type=MESH)

    slab = me // 4 * 4
    up1, down1, up2, down2 = (slab + 4) % 128, (slab + 124) % 128, (slab + 8) % 128, (slab + 120) % 128
    column = {k: (y + k) % 4 for k in (1, 2, 3)}
    greet(me, other)
    for d in (8, 7, 9, 6, 10, 5, 11, 4, 12, 3, 13, 2, 14, 1, 15):
        greet(peer2((z + d) % 16), q - core)
    for d in range(1, 8):
        greet(peer1((spot + d) % 8), q - core + 1)
    for blk in (up1, down1, up2, down2):
        greet(blk + y, q - core)
    for blk in (up1, down1):
        for k in (1, 3):
            greet(blk + column[k], q - core)

    @pl.when(q == 3)
    def _():
        greet((me + 72) % 128, 2)

    @pl.when(core == 1)
    def _():
        pl.semaphore_wait(barrier, 1 + 2 * 7)
        pl.semaphore_signal(near_sem, 1, device_id=device(me, other), device_id_type=MESH)

    loads[4].wait()
    ids = assign[...]
    turned = pltpu.roll(ids, 64, 1)
    rows = [turned] + [pltpu.roll(turned, 8 - k, 0) for k in range(1, 5)]

    def pick(first_row):
        out = rows[first_row + 3]
        for k in (2, 1, 0):
            out = jnp.where(q == k, rows[first_row + k], out)
        return out

    lane = lax.broadcasted_iota(jnp.int32, (8, 128), 1)
    row = lax.broadcasted_iota(jnp.int32, (8, 128), 0)
    moved = jnp.where(lane < 64, pick(0), pick(1))
    wanted = {}
    for yy in range(4):
        index = ((lane >> 3) & 3) * 32 + yy * 8 + (lane & 7)
        got = jnp.take_along_axis(moved, index, axis=1)
        got = jnp.where((lane >> 5) == (row & 3), got, 0)
        for hh in range(2):
            wanted[hh * 4 + yy] = jnp.sum(got[hh * 4 : hh * 4 + 4], axis=0, keepdims=True)

    loads[5].wait()
    samples = series[...].astype(F32)
    for s in range(8):
        source = jnp.broadcast_to(wanted[s] >> 7, (32, 128))
        index = jnp.broadcast_to(wanted[s] & 127, (32, 128))
        part = jnp.zeros((32, 128), F32)
        for k in range(8):
            got = jnp.take_along_axis(samples[:, 128 * k : 128 * k + 128], index, axis=1)
            part = jnp.where(source == k, got, part)
        send1[s] = part.astype(BF16)

    @pl.when(core == 0)
    def _():
        pl.semaphore_wait(near_sem, 1)

    def remote(src, dst, ssem, rsem, blk, pair=None):
        return pltpu.make_async_remote_copy(
            src_ref=src, dst_ref=dst, send_sem=ssem, recv_sem=rsem,
            device_id=device(blk, pair), device_id_type=MESH,
        )

    stage1 = []
    for d in (6, 5, 7, 2, 4, 1, 3):
        s = (spot + d) % 8
        stage1.append(remote(send1.at[s], recv1.at[spot], send1_sem.at[d], recv1_sem.at[d], peer1(s)))
        stage1[-1].start()
    for c in loads[:4]:
        c.start()
    recv1[spot] = send1[spot]

    @pl.when(core == 0)
    def _():
        pl.semaphore_wait(barrier, 1 + 2 * (15 + 4 + 4) + jnp.where(q == 2, 1, 0))
        pl.semaphore_signal(far_sem, 1, device_id=device(me, other), device_id_type=MESH)

    for c in stage1:
        c.wait_recv()
    sides = []
    for hh in range(2):
        side = recv1[hh * 4 : hh * 4 + 4].reshape(128, 128).astype(F32)
        sides.append(jnp.transpose(side).reshape(16, 8, 128))
    send2[...] = jnp.concatenate(sides, axis=1).astype(BF16)

    @pl.when(core == 1)
    def _():
        pl.semaphore_wait(far_sem, 1)

    stage2 = []
    for d in (8, 7, 9, 6, 10, 5, 11, 4, 12, 3, 13, 2, 14, 1, 15):
        zz = (z + d) % 16
        stage2.append(remote(send2.at[zz], recv2.at[z], send2_sem.at[d], recv2_sem.at[d], peer2(zz)))
        stage2[-1].start()
    recv2[z] = send2[z]
    loads[0].wait()
    loads[1].wait()
    loads[2].wait()
    for c in stage2:
        c.wait_recv()

    x = recv2[...].reshape(256, 128)
    a = jnp.dot(first[0], x, preferred_element_type=F32) + jnp.dot(first[1], x, preferred_element_type=F32)
    ac, as_ = a[:256], a[256:]
    tc, ts = twiddle[0], twiddle[1]
    bre, bim = ac * tc - as_ * ts, ac * ts + as_ * tc
    b = jnp.concatenate([v[64 * k : 64 * k + 64] for k in range(4) for v in (bre, bim)], axis=1)
    bhigh = b.astype(BF16)
    blow = (b - bhigh.astype(F32)).astype(BF16)
    both = jnp.dot(jnp.concatenate([bhigh, blow], axis=0), second[0], preferred_element_type=F32)
    spectrum = both[:64] + both[64:] + jnp.dot(bhigh, second[1], preferred_element_type=F32)
    re, im = spectrum[:, :128].reshape(8, 8, 128), spectrum[:, 128:].reshape(8, 8, 128)
    energy = jnp.sum(jnp.sum(re * re + im * im, axis=0), axis=1, keepdims=True)
    scale = lax.rsqrt(energy + 1e-06)
    for k in range(8):
        units[8 + y, :, 128 * k : 128 * k + 128] = jnp.concatenate([re[k] * scale, im[k] * scale], axis=0).astype(BF16)

    mine = units.at[8 + y]
    sent = []

    def send(src, slot, blk, pair=None):
        sem = sendu_sem.at[len(sent)]
        sent.append(remote(src, units.at[slot], sem, recvu_sem.at[slot], blk, pair))
        return sent[-1]

    def arrived(slot):
        remote(mine, units.at[slot], sendu_sem.at[0], recvu_sem.at[slot], (me + 4) % 128).wait_recv()

    to_up2 = send(mine, y, up2 + y)
    to_own = [send(mine, OWN, up2 + y, 1), send(mine, OWN, (me + 56) % 128, 3), send(units.at[OWN], OWN, me, 2)]
    to_down2 = send(mine, PASS, down2 + y)
    send(mine, 8 + y, slab + column[2]).start()
    to_up2.start()

    @pl.when(q == 0)
    def _():
        to_own[0].start()

    @pl.when(q == 3)
    def _():
        to_own[1].start()


    @pl.when(y < 3)
    def _():
        to_down2.start()

    for k in (1, 3):
        send(mine, 8 + y, slab + column[k]).start()
    send(mine, 4 + y, up1 + y).start()
    send(mine, 12 + y, down1 + y).start()
    for k in (1, 3):
        send(mine, 4 + y, up1 + column[k]).start()
        send(mine, 12 + y, down1 + column[k]).start()

    arrived(8 + column[2])
    send(units.at[8 + column[2]], 4 + column[2], up1 + y).start()
    send(units.at[8 + column[2]], 12 + column[2], down1 + y).start()
    arrived(y)

    @pl.when(y < 3)
    def _():
        arrived(PASS)

    for k in (2, 1, 3):
        send(units.at[jnp.where(column[k] < y, y, PASS)], y, slab + column[k]).start()

    @pl.when(q > 0)
    def _():
        arrived(OWN)

    @pl.when(q == 3)
    def _():
        to_own[2].start()

    own_slot = jnp.where(q == 0, y, OWN)
    send(units.at[own_slot], OPP, (me + 64) % 128).start()
    own = units[own_slot].astype(F32)
    for i in range(8):
        for c in range(2):
            wide[c, i] = jnp.broadcast_to(own[8 * c + i : 8 * c + i + 1], (8, 1024))

    def products(slot, spot):
        v = units[slot].astype(F32)
        v0, v1 = v[:8], v[8:]
        for i in range(0, 8, 2):
            real = [wide[0, i + j] * v0 + wide[1, i + j] * v1 for j in range(2)]
            imag = [wide[1, i + j] * v0 - wide[0, i + j] * v1 for j in range(2)]
            lhs[spot, 8 * i : 8 * i + 16, :1024] = jnp.concatenate(real, axis=0).astype(BF16)
            lhs[spot, 8 * i : 8 * i + 16, 1024:] = jnp.concatenate(imag, axis=0).astype(BF16)

    def correlate(first_spot, slots):
        for k, slot in enumerate(slots):
            products(slot, first_spot + k)
        rows = lhs[first_spot : first_spot + len(slots)].reshape(64 * len(slots), 2048)
        out = jnp.dot(rows, lag[...], preferred_element_type=F32)
        for k, slot in enumerate(slots):
            if not isinstance(slot, int) or slot != OPP:
                cross[(slot - y + 16) % 16] = out[64 * k : 64 * k + 64]
        return out

    loads[3].wait()
    arrived(8 + column[1])
    arrived(8 + column[3])
    correlate(0, [8, 9, 10, 11])
    near = [first + c for first in (4, 12) for c in (y, column[1], column[3])]
    for slot in near:
        arrived(slot)
    correlate(4, [y] + near)
    late = [4 + column[2], 12 + column[2]]
    for slot in late + [OPP]:
        arrived(slot)
    far = correlate(11, late + [OPP])[128:]
    out = far[:, 192:]
    for k in range(3):
        out = jnp.where(q == k, far[:, 64 * k : 64 * k + 64], out)
    opposite[...] = out
    edges = [column[k] for k in (1, 2, 3)]
    for slot in edges:
        arrived(slot)
    correlate(14, edges)

    for c in stage1 + stage2:
        c.wait_send()
    special = [id(c) for c in [to_down2] + to_own]
    for c in sent:
        if id(c) not in special:
            c.wait_send()

    @pl.when(y < 3)
    def _():
        to_down2.wait_send()

    @pl.when(q == 0)
    def _():
        to_own[0].wait_send()

    @pl.when(q == 3)
    def _():
        to_own[1].wait_send()
        to_own[2].wait_send()


def finish(cross, opposite, cross_out, opposite_out, sem):
    copies = [
        pltpu.make_async_copy(cross, cross_out, sem.at[0]),
        pltpu.make_async_copy(opposite, opposite_out, sem.at[1]),
    ]
    for c in copies:
        c.start()
    for c in copies:
        c.wait()


def body(series, assign):
    first, twiddle, second, lag = tables()
    vmem = pl.BlockSpec(memory_space=pltpu.VMEM)
    hbm = pl.BlockSpec(memory_space=pltpu.HBM)
    dma = pltpu.SemaphoreType.DMA
    cross, opposite = pl.pallas_call(
        kernel,
        out_shape=[pltpu.VMEM((16, 64, 256), F32), pltpu.VMEM((64, 64), F32)],
        in_specs=[hbm] * 6,
        out_specs=[vmem] * 2,
        scratch_shapes=[
            pltpu.VMEM((32, 1024), BF16),
            pltpu.VMEM((8, 128), jnp.int32),
            pltpu.VMEM(first.shape, BF16),
            pltpu.VMEM(twiddle.shape, F32),
            pltpu.VMEM(second.shape, BF16),
            pltpu.VMEM(lag.shape, BF16),
            pltpu.VMEM((8, 32, 128), BF16),
            pltpu.VMEM((8, 32, 128), BF16),
            pltpu.VMEM((16, 16, 128), BF16),
            pltpu.VMEM((16, 16, 128), BF16),
            pltpu.VMEM((19, 16, 1024), BF16),
            pltpu.VMEM((2, 8, 8, 1024), F32),
            pltpu.VMEM((17, 64, 2048), BF16),
            dma((6,)), dma((8,)), dma((8,)), dma((16,)), dma((16,)), dma((23,)), dma((19,)),
            pltpu.SemaphoreType.REGULAR, pltpu.SemaphoreType.REGULAR,
        ],
        compiler_params=pltpu.CompilerParams(
            collective_id=0, has_side_effects=True, vmem_limit_bytes=60 * 1024 * 1024
        ),
    )(series.T, assign.reshape(8, 128), first, twiddle, second, lag)
    cross, opposite = pl.pallas_call(
        finish,
        out_shape=[jax.ShapeDtypeStruct((16, 64, 256), F32), jax.ShapeDtypeStruct((64, 64), F32)],
        in_specs=[vmem] * 2,
        out_specs=[pl.BlockSpec(memory_space=pltpu.HBM)] * 2,
        scratch_shapes=[dma((2,))],
        compiler_params=pltpu.CompilerParams(vmem_limit_bytes=2 * 1024 * 1024),
    )(cross, opposite)
    return cross.reshape(1, 1, 16, 8, 8, 256), opposite.reshape(1, 8, 8, 64)


def solution(mesh):
    in_specs = (P(None, "blk"), P())
    out_specs = (P("blk", "pair", None, None, None, None), P("blk", None, None, "pair"))
    return jax.shard_map(body, mesh=mesh, in_specs=in_specs, out_specs=out_specs, check_vma=False)
```

```python
import math

import jax
import jax.numpy as jnp
import ml_dtypes
import numpy as np
from jax import lax
from jax.experimental import pallas as pl
from jax.experimental.pallas import tpu as pltpu
from jax.sharding import PartitionSpec as P

F32 = jnp.float32
BF16 = jnp.bfloat16
MESH = pl.DeviceIdType.MESH
N = 4096
PASS, OWN, OPP = 16, 17, 18


def two_parts(x):
    high = x.astype(ml_dtypes.bfloat16)
    low = (x - high.astype(np.float64)).astype(ml_dtypes.bfloat16)
    return np.stack([high, low])


def tables():
    k1 = np.arange(32)
    z, h = np.arange(16), np.arange(2)
    n1 = 16 * h[None, :] + z[:, None]
    angle = 2 * np.pi * ((k1[:, None, None] + 1) * n1[None] % 32) / 32
    first = np.stack([np.cos(angle), np.sin(angle)]) / math.sqrt(N)
    first = np.einsum("ckzh,pr->ckpzhr", first, np.eye(8)).reshape(512, 256)
    n2 = np.arange(128)
    angle = 2 * np.pi * ((k1[:, None] + 1) * n2[None] % N) / N
    twiddle = np.stack([np.cos(angle), np.sin(angle)])
    twiddle = np.repeat(twiddle, 8, axis=1).astype(np.float32)
    k2 = np.arange(32)
    angle = 2 * np.pi * (n2[:, None] * k2[None] % 128) / 128
    co, si = np.cos(angle), np.sin(angle)
    second = np.array([[co, si], [-si, co]])
    second = np.einsum("rcnk,ab->arncbk", second, np.eye(4)).reshape(1024, 256)
    k1b, k1a = np.arange(8), np.arange(4)
    k = 1 + 8 * k1a[None, :, None] + k1b[:, None, None] + 32 * k2[None, None, :]
    shift = np.arange(256) - 128
    angle = 2 * np.pi * (k.reshape(1024)[:, None] * shift[None] % N) / N
    lag = np.concatenate([np.cos(angle), -np.sin(angle)]).astype(ml_dtypes.bfloat16)
    return two_parts(first), twiddle, two_parts(second), lag


def kernel(
    series_hbm, assign_hbm, first_hbm, twiddle_hbm, second_hbm, lag_hbm,
    cross, opposite,
    series, assign, first, twiddle, second, lag, send1, recv1, send2, recv2, units, wide, lhs,
    load_sem, send1_sem, recv1_sem, send2_sem, recv2_sem, sendu_sem, recvu_sem, near_sem, far_sem,
):
    me, q = lax.axis_index("blk"), lax.axis_index("pair")
    half, z, y = me // 64, me // 4 % 16, me % 4
    spot = half * 4 + y

    def device(blk, pair=None):
        return {"blk": blk, "pair": q if pair is None else pair}

    def peer1(s):
        return s // 4 * 64 + z * 4 + s % 4

    def peer2(zz):
        return half * 64 + zz * 4 + y

    loads = [
        pltpu.make_async_copy(src, dst, load_sem.at[i])
        for i, (src, dst) in enumerate(
            [(first_hbm, first), (twiddle_hbm, twiddle), (second_hbm, second), (lag_hbm, lag),
             (assign_hbm, assign), (series_hbm, series)]
        )
    ]
    for c in loads[4:]:
        c.start()

    barrier = pltpu.get_barrier_semaphore()
    core = q % 2
    other = q + 1 - 2 * core

    def greet(blk, pair):
        pl.semaphore_signal(barrier, 1, device_id=device(blk, pair), device_id_type=MESH)

    slab = me // 4 * 4
    up1, down1, up2, down2 = (slab + 4) % 128, (slab + 124) % 128, (slab + 8) % 128, (slab + 120) % 128
    column = {k: (y + k) % 4 for k in (1, 2, 3)}
    greet(me, other)
    for d in (8, 7, 9, 6, 10, 5, 11, 4, 12, 3, 13, 2, 14, 1, 15):
        greet(peer2((z + d) % 16), q - core)
    for d in range(1, 8):
        greet(peer1((spot + d) % 8), q - core + 1)
    for blk, wraps in ((up1, z == 15), (down1, z == 0), (up2, z >= 14), (down2, z <= 1)):
        pl.when(wraps)(lambda blk=blk: greet(blk + y, q - core))
    for blk in (up1, down1):
        for k in (1, 3):
            greet(blk + column[k], q - core)

    @pl.when(q == 3)
    def _():
        greet((me + 72) % 128, 2)

    @pl.when(core == 1)
    def _():
        pl.semaphore_wait(barrier, 1 + 2 * 7)
        pl.semaphore_signal(near_sem, 1, device_id=device(me, other), device_id_type=MESH)

    loads[4].wait()
    ids = assign[...]
    turned = pltpu.roll(ids, 64, 1)
    rows = [turned] + [pltpu.roll(turned, 8 - k, 0) for k in range(1, 5)]

    def pick(first_row):
        out = rows[first_row + 3]
        for k in (2, 1, 0):
            out = jnp.where(q == k, rows[first_row + k], out)
        return out

    lane = lax.broadcasted_iota(jnp.int32, (8, 128), 1)
    row = lax.broadcasted_iota(jnp.int32, (8, 128), 0)
    moved = jnp.where(lane < 64, pick(0), pick(1))
    wanted = {}
    for yy in range(4):
        index = ((lane >> 3) & 3) * 32 + yy * 8 + (lane & 7)
        got = jnp.take_along_axis(moved, index, axis=1)
        got = jnp.where((lane >> 5) == (row & 3), got, 0)
        for hh in range(2):
            wanted[hh * 4 + yy] = jnp.sum(got[hh * 4 : hh * 4 + 4], axis=0, keepdims=True)

    loads[5].wait()
    samples = series[...].astype(F32)
    for s in range(8):
        source = jnp.broadcast_to(wanted[s] >> 7, (32, 128))
        index = jnp.broadcast_to(wanted[s] & 127, (32, 128))
        part = jnp.zeros((32, 128), F32)
        for k in range(8):
            got = jnp.take_along_axis(samples[:, 128 * k : 128 * k + 128], index, axis=1)
            part = jnp.where(source == k, got, part)
        send1[s] = part.astype(BF16)

    @pl.when(core == 0)
    def _():
        pl.semaphore_wait(near_sem, 1)

    def remote(src, dst, ssem, rsem, blk, pair=None):
        return pltpu.make_async_remote_copy(
            src_ref=src, dst_ref=dst, send_sem=ssem, recv_sem=rsem,
            device_id=device(blk, pair), device_id_type=MESH,
        )

    stage1 = []
    for d in (6, 5, 7, 2, 4, 1, 3):
        s = (spot + d) % 8
        stage1.append(remote(send1.at[s], recv1.at[spot], send1_sem.at[d], recv1_sem.at[d], peer1(s)))
        stage1[-1].start()
    for c in loads[:4]:
        c.start()
    recv1[spot] = send1[spot]

    @pl.when(core == 0)
    def _():
        pl.semaphore_wait(barrier, 1 + 2 * (15 + 4 + jnp.where(jnp.logical_or(z == 0, z == 15), 2, jnp.where(jnp.logical_or(z == 1, z == 14), 1, 0))) + jnp.where(q == 2, 1, 0))
        pl.semaphore_signal(far_sem, 1, device_id=device(me, other), device_id_type=MESH)

    for c in stage1:
        c.wait_recv()
    sides = []
    for hh in range(2):
        side = recv1[hh * 4 : hh * 4 + 4].reshape(128, 128).astype(F32)
        sides.append(jnp.transpose(side).reshape(16, 8, 128))
    send2[...] = jnp.concatenate(sides, axis=1).astype(BF16)

    @pl.when(core == 1)
    def _():
        pl.semaphore_wait(far_sem, 1)

    stage2 = []
    for d in (8, 7, 9, 6, 10, 5, 11, 4, 12, 3, 13, 2, 14, 1, 15):
        zz = (z + d) % 16
        stage2.append(remote(send2.at[zz], recv2.at[z], send2_sem.at[d], recv2_sem.at[d], peer2(zz)))
        stage2[-1].start()
    recv2[z] = send2[z]
    loads[0].wait()
    loads[1].wait()
    loads[2].wait()
    for c in stage2:
        c.wait_recv()

    x = recv2[...].reshape(256, 128)
    a = jnp.dot(first[0], x, preferred_element_type=F32) + jnp.dot(first[1], x, preferred_element_type=F32)
    ac, as_ = a[:256], a[256:]
    tc, ts = twiddle[0], twiddle[1]
    bre, bim = ac * tc - as_ * ts, ac * ts + as_ * tc
    b = jnp.concatenate([v[64 * k : 64 * k + 64] for k in range(4) for v in (bre, bim)], axis=1)
    bhigh = b.astype(BF16)
    blow = (b - bhigh.astype(F32)).astype(BF16)
    both = jnp.dot(jnp.concatenate([bhigh, blow], axis=0), second[0], preferred_element_type=F32)
    spectrum = both[:64] + both[64:] + jnp.dot(bhigh, second[1], preferred_element_type=F32)
    re, im = spectrum[:, :128].reshape(8, 8, 128), spectrum[:, 128:].reshape(8, 8, 128)
    energy = jnp.sum(jnp.sum(re * re + im * im, axis=0), axis=1, keepdims=True)
    scale = lax.rsqrt(energy + 1e-06)
    for k in range(8):
        units[8 + y, :, 128 * k : 128 * k + 128] = jnp.concatenate([re[k] * scale, im[k] * scale], axis=0).astype(BF16)

    mine = units.at[8 + y]
    sent = []

    def send(src, slot, blk, pair=None):
        sem = sendu_sem.at[len(sent)]
        sent.append(remote(src, units.at[slot], sem, recvu_sem.at[slot], blk, pair))
        return sent[-1]

    def arrived(slot):
        remote(mine, units.at[slot], sendu_sem.at[0], recvu_sem.at[slot], (me + 4) % 128).wait_recv()

    to_up2 = send(mine, y, up2 + y)
    to_own = [send(mine, OWN, up2 + y, 1), send(mine, OWN, (me + 56) % 128, 3), send(units.at[OWN], OWN, me, 2)]
    to_down2 = send(mine, PASS, down2 + y)
    send(mine, 8 + y, slab + column[2]).start()
    to_up2.start()

    @pl.when(q == 0)
    def _():
        to_own[0].start()

    @pl.when(q == 3)
    def _():
        to_own[1].start()


    @pl.when(y < 3)
    def _():
        to_down2.start()

    for k in (1, 3):
        send(mine, 8 + y, slab + column[k]).start()
    send(mine, 4 + y, up1 + y).start()
    send(mine, 12 + y, down1 + y).start()
    for first, blk in ((4, up1), (12, down1)):
        for k in (1, 3):
            send(mine, first + y, blk + column[k]).start()

    arrived(8 + column[2])
    send(units.at[8 + column[2]], 4 + column[2], up1 + y).start()
    send(units.at[8 + column[2]], 12 + column[2], down1 + y).start()
    arrived(y)

    @pl.when(y < 3)
    def _():
        arrived(PASS)

    for k in (2, 1, 3):
        send(units.at[jnp.where(column[k] < y, y, PASS)], y, slab + column[k]).start()

    @pl.when(q > 0)
    def _():
        arrived(OWN)

    @pl.when(q == 3)
    def _():
        to_own[2].start()

    own_slot = jnp.where(q == 0, y, OWN)
    send(units.at[own_slot], OPP, (me + 64) % 128).start()
    own = units[own_slot].astype(F32)
    for i in range(8):
        for c in range(2):
            wide[c, i] = jnp.broadcast_to(own[8 * c + i : 8 * c + i + 1], (8, 1024))

    def products(slot, spot):
        v = units[slot].astype(F32)
        v0, v1 = v[:8], v[8:]
        for i in range(0, 8, 2):
            real = [wide[0, i + j] * v0 + wide[1, i + j] * v1 for j in range(2)]
            imag = [wide[1, i + j] * v0 - wide[0, i + j] * v1 for j in range(2)]
            lhs[spot, 8 * i : 8 * i + 16, :1024] = jnp.concatenate(real, axis=0).astype(BF16)
            lhs[spot, 8 * i : 8 * i + 16, 1024:] = jnp.concatenate(imag, axis=0).astype(BF16)

    def correlate(first_spot, slots):
        for k, slot in enumerate(slots):
            products(slot, first_spot + k)
        rows = lhs[first_spot : first_spot + len(slots)].reshape(64 * len(slots), 2048)
        out = jnp.dot(rows, lag[...], preferred_element_type=F32)
        for k, slot in enumerate(slots):
            if not isinstance(slot, int) or slot != OPP:
                cross[(slot - y + 16) % 16] = out[64 * k : 64 * k + 64]
        return out

    loads[3].wait()
    arrived(8 + column[1])
    arrived(8 + column[3])
    correlate(0, [8, 9, 10, 11])
    near = [first + c for first in (4, 12) for c in (y, column[1], column[3])]
    for slot in near:
        arrived(slot)
    correlate(4, [y] + near)
    late = [4 + column[2], 12 + column[2]]
    for slot in late + [OPP]:
        arrived(slot)
    far = correlate(11, late + [OPP])[128:]
    out = far[:, 192:]
    for k in range(3):
        out = jnp.where(q == k, far[:, 64 * k : 64 * k + 64], out)
    opposite[...] = out
    edges = [column[k] for k in (1, 2, 3)]
    for slot in edges:
        arrived(slot)
    correlate(14, edges)

    for c in stage1 + stage2:
        c.wait_send()
    special = [id(c) for c in [to_down2] + to_own]
    for c in sent:
        if id(c) not in special:
            c.wait_send()

    @pl.when(y < 3)
    def _():
        to_down2.wait_send()

    @pl.when(q == 0)
    def _():
        to_own[0].wait_send()

    @pl.when(q == 3)
    def _():
        to_own[1].wait_send()
        to_own[2].wait_send()


def finish(cross, opposite, cross_out, opposite_out, sem):
    copies = [
        pltpu.make_async_copy(cross, cross_out, sem.at[0]),
        pltpu.make_async_copy(opposite, opposite_out, sem.at[1]),
    ]
    for c in copies:
        c.start()
    for c in copies:
        c.wait()


def body(series, assign):
    first, twiddle, second, lag = tables()
    vmem = pl.BlockSpec(memory_space=pltpu.VMEM)
    hbm = pl.BlockSpec(memory_space=pltpu.HBM)
    dma = pltpu.SemaphoreType.DMA
    cross, opposite = pl.pallas_call(
        kernel,
        out_shape=[pltpu.VMEM((16, 64, 256), F32), pltpu.VMEM((64, 64), F32)],
        in_specs=[hbm] * 6,
        out_specs=[vmem] * 2,
        scratch_shapes=[
            pltpu.VMEM((32, 1024), BF16),
            pltpu.VMEM((8, 128), jnp.int32),
            pltpu.VMEM(first.shape, BF16),
            pltpu.VMEM(twiddle.shape, F32),
            pltpu.VMEM(second.shape, BF16),
            pltpu.VMEM(lag.shape, BF16),
            pltpu.VMEM((8, 32, 128), BF16),
            pltpu.VMEM((8, 32, 128), BF16),
            pltpu.VMEM((16, 16, 128), BF16),
            pltpu.VMEM((16, 16, 128), BF16),
            pltpu.VMEM((19, 16, 1024), BF16),
            pltpu.VMEM((2, 8, 8, 1024), F32),
            pltpu.VMEM((17, 64, 2048), BF16),
            dma((6,)), dma((8,)), dma((8,)), dma((16,)), dma((16,)), dma((23,)), dma((19,)),
            pltpu.SemaphoreType.REGULAR, pltpu.SemaphoreType.REGULAR,
        ],
        compiler_params=pltpu.CompilerParams(
            collective_id=0, has_side_effects=True, vmem_limit_bytes=60 * 1024 * 1024
        ),
    )(series.T, assign.reshape(8, 128), first, twiddle, second, lag)
    cross, opposite = pl.pallas_call(
        finish,
        out_shape=[jax.ShapeDtypeStruct((16, 64, 256), F32), jax.ShapeDtypeStruct((64, 64), F32)],
        in_specs=[vmem] * 2,
        out_specs=[pl.BlockSpec(memory_space=pltpu.HBM)] * 2,
        scratch_shapes=[dma((2,))],
        compiler_params=pltpu.CompilerParams(vmem_limit_bytes=2 * 1024 * 1024),
    )(cross, opposite)
    return cross.reshape(1, 1, 16, 8, 8, 256), opposite.reshape(1, 8, 8, 64)


def solution(mesh):
    in_specs = (P(None, "blk"), P())
    out_specs = (P("blk", "pair", None, None, None, None), P("blk", None, None, "pair"))
    return jax.shard_map(body, mesh=mesh, in_specs=in_specs, out_specs=out_specs, check_vma=False)
```

```python
import math

import jax
import jax.numpy as jnp
import ml_dtypes
import numpy as np
from jax import lax
from jax.experimental import pallas as pl
from jax.experimental.pallas import tpu as pltpu
from jax.sharding import PartitionSpec as P

F32 = jnp.float32
BF16 = jnp.bfloat16
MESH = pl.DeviceIdType.MESH
N = 4096
PASS, OWN, OPP = 16, 17, 18


def two_parts(x):
    high = x.astype(ml_dtypes.bfloat16)
    low = (x - high.astype(np.float64)).astype(ml_dtypes.bfloat16)
    return np.stack([high, low])


def tables():
    k1 = np.arange(32)
    z, h = np.arange(16), np.arange(2)
    n1 = 16 * h[None, :] + z[:, None]
    angle = 2 * np.pi * ((k1[:, None, None] + 1) * n1[None] % 32) / 32
    first = np.stack([np.cos(angle), np.sin(angle)]) / math.sqrt(N)
    first = np.einsum("ckzh,pr->ckpzhr", first, np.eye(8)).reshape(512, 256)
    n2 = np.arange(128)
    angle = 2 * np.pi * ((k1[:, None] + 1) * n2[None] % N) / N
    twiddle = np.stack([np.cos(angle), np.sin(angle)])
    twiddle = np.repeat(twiddle, 8, axis=1).astype(np.float32)
    k2 = np.arange(32)
    angle = 2 * np.pi * (n2[:, None] * k2[None] % 128) / 128
    co, si = np.cos(angle), np.sin(angle)
    second = np.array([[co, si], [-si, co]])
    second = np.einsum("rcnk,ab->arncbk", second, np.eye(4)).reshape(1024, 256)
    k1b, k1a = np.arange(8), np.arange(4)
    k = 1 + 8 * k1a[None, :, None] + k1b[:, None, None] + 32 * k2[None, None, :]
    shift = np.arange(256) - 128
    angle = 2 * np.pi * (k.reshape(1024)[:, None] * shift[None] % N) / N
    lag = np.concatenate([np.cos(angle), -np.sin(angle)]).astype(ml_dtypes.bfloat16)
    return two_parts(first), twiddle, two_parts(second), lag


def kernel(
    series_hbm, assign_hbm, first_hbm, twiddle_hbm, second_hbm, lag_hbm,
    cross, opposite,
    series, assign, first, twiddle, second, lag, send1, recv1, send2, recv2, units, wide, lhs,
    load_sem, send1_sem, recv1_sem, send2_sem, recv2_sem, sendu_sem, recvu_sem, near_sem, far_sem,
):
    me, q = lax.axis_index("blk"), lax.axis_index("pair")
    half, z, y = me // 64, me // 4 % 16, me % 4
    spot = half * 4 + y

    def device(blk, pair=None):
        return {"blk": blk, "pair": q if pair is None else pair}

    def peer1(s):
        return s // 4 * 64 + z * 4 + s % 4

    def peer2(zz):
        return half * 64 + zz * 4 + y

    loads = [
        pltpu.make_async_copy(src, dst, load_sem.at[i])
        for i, (src, dst) in enumerate(
            [(first_hbm, first), (twiddle_hbm, twiddle), (second_hbm, second), (lag_hbm, lag),
             (assign_hbm, assign), (series_hbm, series)]
        )
    ]
    for c in loads[4:]:
        c.start()

    barrier = pltpu.get_barrier_semaphore()
    core = q % 2
    other = q + 1 - 2 * core

    def greet(blk, pair):
        pl.semaphore_signal(barrier, 1, device_id=device(blk, pair), device_id_type=MESH)

    slab = me // 4 * 4
    up1, down1, up2, down2 = (slab + 4) % 128, (slab + 124) % 128, (slab + 8) % 128, (slab + 120) % 128
    column = {k: (y + k) % 4 for k in (1, 2, 3)}
    greet(me, other)
    for d in range(1, 8):
        greet(peer1((spot + d) % 8), q - core + 1)
    for d in (8, 7, 9, 6, 10, 5, 11, 4, 12, 3, 13, 2, 14, 1, 15):
        greet(peer2((z + d) % 16), q - core)
    for blk in (up1, down1, up2, down2):
        greet(blk + y, q - core)
    for blk in (up1, down1):
        for k in (1, 3):
            greet(blk + column[k], q - core)

    @pl.when(q == 3)
    def _():
        greet((me + 72) % 128, 2)

    @pl.when(core == 1)
    def _():
        pl.semaphore_wait(barrier, 1 + 2 * 7)
        pl.semaphore_signal(near_sem, 1, device_id=device(me, other), device_id_type=MESH)

    loads[4].wait()
    ids = assign[...]
    turned = pltpu.roll(ids, 64, 1)
    rows = [turned] + [pltpu.roll(turned, 8 - k, 0) for k in range(1, 5)]

    def pick(first_row):
        out = rows[first_row + 3]
        for k in (2, 1, 0):
            out = jnp.where(q == k, rows[first_row + k], out)
        return out

    lane = lax.broadcasted_iota(jnp.int32, (8, 128), 1)
    row = lax.broadcasted_iota(jnp.int32, (8, 128), 0)
    moved = jnp.where(lane < 64, pick(0), pick(1))
    wanted = {}
    for yy in range(4):
        index = ((lane >> 3) & 3) * 32 + yy * 8 + (lane & 7)
        got = jnp.take_along_axis(moved, index, axis=1)
        got = jnp.where((lane >> 5) == (row & 3), got, 0)
        for hh in range(2):
            wanted[hh * 4 + yy] = jnp.sum(got[hh * 4 : hh * 4 + 4], axis=0, keepdims=True)

    loads[5].wait()
    samples = series[...].astype(F32)
    for s in range(8):
        source = jnp.broadcast_to(wanted[s] >> 7, (32, 128))
        index = jnp.broadcast_to(wanted[s] & 127, (32, 128))
        part = jnp.zeros((32, 128), F32)
        for k in range(8):
            got = jnp.take_along_axis(samples[:, 128 * k : 128 * k + 128], index, axis=1)
            part = jnp.where(source == k, got, part)
        send1[s] = part.astype(BF16)

    @pl.when(core == 0)
    def _():
        pl.semaphore_wait(near_sem, 1)

    def remote(src, dst, ssem, rsem, blk, pair=None):
        return pltpu.make_async_remote_copy(
            src_ref=src, dst_ref=dst, send_sem=ssem, recv_sem=rsem,
            device_id=device(blk, pair), device_id_type=MESH,
        )

    stage1 = []
    for d in (6, 5, 7, 2, 4, 1, 3):
        s = (spot + d) % 8
        stage1.append(remote(send1.at[s], recv1.at[spot], send1_sem.at[d], recv1_sem.at[d], peer1(s)))
        stage1[-1].start()
    for c in loads[:4]:
        c.start()
    recv1[spot] = send1[spot]

    @pl.when(core == 0)
    def _():
        pl.semaphore_wait(barrier, 1 + 2 * (15 + 4 + 4) + jnp.where(q == 2, 1, 0))
        pl.semaphore_signal(far_sem, 1, device_id=device(me, other), device_id_type=MESH)

    for c in stage1:
        c.wait_recv()
    sides = []
    for hh in range(2):
        side = recv1[hh * 4 : hh * 4 + 4].reshape(128, 128).astype(F32)
        sides.append(jnp.transpose(side).reshape(16, 8, 128))
    send2[...] = jnp.concatenate(sides, axis=1).astype(BF16)

    @pl.when(core == 1)
    def _():
        pl.semaphore_wait(far_sem, 1)

    stage2 = []
    for d in (8, 7, 9, 6, 10, 5, 11, 4, 12, 3, 13, 2, 14, 1, 15):
        zz = (z + d) % 16
        stage2.append(remote(send2.at[zz], recv2.at[z], send2_sem.at[d], recv2_sem.at[d], peer2(zz)))
        stage2[-1].start()
    recv2[z] = send2[z]
    loads[0].wait()
    loads[1].wait()
    loads[2].wait()
    for c in stage2:
        c.wait_recv()

    x = recv2[...].reshape(256, 128)
    a = jnp.dot(first[0], x, preferred_element_type=F32) + jnp.dot(first[1], x, preferred_element_type=F32)
    ac, as_ = a[:256], a[256:]
    tc, ts = twiddle[0], twiddle[1]
    bre, bim = ac * tc - as_ * ts, ac * ts + as_ * tc
    b = jnp.concatenate([v[64 * k : 64 * k + 64] for k in range(4) for v in (bre, bim)], axis=1)
    bhigh = b.astype(BF16)
    blow = (b - bhigh.astype(F32)).astype(BF16)
    both = jnp.dot(jnp.concatenate([bhigh, blow], axis=0), second[0], preferred_element_type=F32)
    spectrum = both[:64] + both[64:] + jnp.dot(bhigh, second[1], preferred_element_type=F32)
    re, im = spectrum[:, :128].reshape(8, 8, 128), spectrum[:, 128:].reshape(8, 8, 128)
    energy = jnp.sum(jnp.sum(re * re + im * im, axis=0), axis=1, keepdims=True)
    scale = lax.rsqrt(energy + 1e-06)
    for k in range(8):
        units[8 + y, :, 128 * k : 128 * k + 128] = jnp.concatenate([re[k] * scale, im[k] * scale], axis=0).astype(BF16)

    mine = units.at[8 + y]
    sent = []

    def send(src, slot, blk, pair=None):
        sem = sendu_sem.at[len(sent)]
        sent.append(remote(src, units.at[slot], sem, recvu_sem.at[slot], blk, pair))
        return sent[-1]

    def arrived(slot):
        remote(mine, units.at[slot], sendu_sem.at[0], recvu_sem.at[slot], (me + 4) % 128).wait_recv()

    to_up2 = send(mine, y, up2 + y)
    to_own = [send(mine, OWN, up2 + y, 1), send(mine, OWN, (me + 56) % 128, 3), send(units.at[OWN], OWN, me, 2)]
    to_down2 = send(mine, PASS, down2 + y)
    send(mine, 8 + y, slab + column[2]).start()
    to_up2.start()

    @pl.when(q == 0)
    def _():
        to_own[0].start()

    @pl.when(q == 3)
    def _():
        to_own[1].start()


    @pl.when(y < 3)
    def _():
        to_down2.start()

    for k in (1, 3):
        send(mine, 8 + y, slab + column[k]).start()
    send(mine, 4 + y, up1 + y).start()
    send(mine, 12 + y, down1 + y).start()
    for k in (1, 3):
        send(mine, 4 + y, up1 + column[k]).start()
        send(mine, 12 + y, down1 + column[k]).start()

    arrived(8 + column[2])
    send(units.at[8 + column[2]], 4 + column[2], up1 + y).start()
    send(units.at[8 + column[2]], 12 + column[2], down1 + y).start()
    arrived(y)

    @pl.when(y < 3)
    def _():
        arrived(PASS)

    for k in (2, 1, 3):
        send(units.at[jnp.where(column[k] < y, y, PASS)], y, slab + column[k]).start()

    @pl.when(q > 0)
    def _():
        arrived(OWN)

    @pl.when(q == 3)
    def _():
        to_own[2].start()

    own_slot = jnp.where(q == 0, y, OWN)
    send(units.at[own_slot], OPP, (me + 64) % 128).start()
    own = units[own_slot].astype(F32)
    for i in range(8):
        for c in range(2):
            wide[c, i] = jnp.broadcast_to(own[8 * c + i : 8 * c + i + 1], (8, 1024))

    def products(slot, spot):
        v = units[slot].astype(F32)
        v0, v1 = v[:8], v[8:]
        for i in range(0, 8, 2):
            real = [wide[0, i + j] * v0 + wide[1, i + j] * v1 for j in range(2)]
            imag = [wide[1, i + j] * v0 - wide[0, i + j] * v1 for j in range(2)]
            lhs[spot, 8 * i : 8 * i + 16, :1024] = jnp.concatenate(real, axis=0).astype(BF16)
            lhs[spot, 8 * i : 8 * i + 16, 1024:] = jnp.concatenate(imag, axis=0).astype(BF16)

    def correlate(first_spot, slots):
        for k, slot in enumerate(slots):
            products(slot, first_spot + k)
        rows = lhs[first_spot : first_spot + len(slots)].reshape(64 * len(slots), 2048)
        out = jnp.dot(rows, lag[...], preferred_element_type=F32)
        for k, slot in enumerate(slots):
            if not isinstance(slot, int) or slot != OPP:
                cross[(slot - y + 16) % 16] = out[64 * k : 64 * k + 64]
        return out

    loads[3].wait()
    arrived(8 + column[1])
    arrived(8 + column[3])
    correlate(0, [8, 9, 10, 11])
    near = [first + c for first in (4, 12) for c in (y, column[1], column[3])]
    for slot in near:
        arrived(slot)
    correlate(4, [y] + near)
    late = [4 + column[2], 12 + column[2]]
    for slot in late + [OPP]:
        arrived(slot)
    far = correlate(11, late + [OPP])[128:]
    out = far[:, 192:]
    for k in range(3):
        out = jnp.where(q == k, far[:, 64 * k : 64 * k + 64], out)
    opposite[...] = out
    edges = [column[k] for k in (1, 2, 3)]
    for slot in edges:
        arrived(slot)
    correlate(14, edges)

    for c in stage1 + stage2:
        c.wait_send()
    special = [id(c) for c in [to_down2] + to_own]
    for c in sent:
        if id(c) not in special:
            c.wait_send()

    @pl.when(y < 3)
    def _():
        to_down2.wait_send()

    @pl.when(q == 0)
    def _():
        to_own[0].wait_send()

    @pl.when(q == 3)
    def _():
        to_own[1].wait_send()
        to_own[2].wait_send()


def finish(cross, opposite, cross_out, opposite_out, sem):
    copies = [
        pltpu.make_async_copy(cross, cross_out, sem.at[0]),
        pltpu.make_async_copy(opposite, opposite_out, sem.at[1]),
    ]
    for c in copies:
        c.start()
    for c in copies:
        c.wait()


def body(series, assign):
    first, twiddle, second, lag = tables()
    vmem = pl.BlockSpec(memory_space=pltpu.VMEM)
    hbm = pl.BlockSpec(memory_space=pltpu.HBM)
    dma = pltpu.SemaphoreType.DMA
    cross, opposite = pl.pallas_call(
        kernel,
        out_shape=[pltpu.VMEM((16, 64, 256), F32), pltpu.VMEM((64, 64), F32)],
        in_specs=[hbm] * 6,
        out_specs=[vmem] * 2,
        scratch_shapes=[
            pltpu.VMEM((32, 1024), BF16),
            pltpu.VMEM((8, 128), jnp.int32),
            pltpu.VMEM(first.shape, BF16),
            pltpu.VMEM(twiddle.shape, F32),
            pltpu.VMEM(second.shape, BF16),
            pltpu.VMEM(lag.shape, BF16),
            pltpu.VMEM((8, 32, 128), BF16),
            pltpu.VMEM((8, 32, 128), BF16),
            pltpu.VMEM((16, 16, 128), BF16),
            pltpu.VMEM((16, 16, 128), BF16),
            pltpu.VMEM((19, 16, 1024), BF16),
            pltpu.VMEM((2, 8, 8, 1024), F32),
            pltpu.VMEM((17, 64, 2048), BF16),
            dma((6,)), dma((8,)), dma((8,)), dma((16,)), dma((16,)), dma((23,)), dma((19,)),
            pltpu.SemaphoreType.REGULAR, pltpu.SemaphoreType.REGULAR,
        ],
        compiler_params=pltpu.CompilerParams(
            collective_id=0, has_side_effects=True, vmem_limit_bytes=60 * 1024 * 1024
        ),
    )(series.T, assign.reshape(8, 128), first, twiddle, second, lag)
    cross, opposite = pl.pallas_call(
        finish,
        out_shape=[jax.ShapeDtypeStruct((16, 64, 256), F32), jax.ShapeDtypeStruct((64, 64), F32)],
        in_specs=[vmem] * 2,
        out_specs=[pl.BlockSpec(memory_space=pltpu.HBM)] * 2,
        scratch_shapes=[dma((2,))],
        compiler_params=pltpu.CompilerParams(vmem_limit_bytes=2 * 1024 * 1024),
    )(cross, opposite)
    return cross.reshape(1, 1, 16, 8, 8, 256), opposite.reshape(1, 8, 8, 64)


def solution(mesh):
    in_specs = (P(None, "blk"), P())
    out_specs = (P("blk", "pair", None, None, None, None), P("blk", None, None, "pair"))
    return jax.shard_map(body, mesh=mesh, in_specs=in_specs, out_specs=out_specs, check_vma=False)
```
